256 devices in a mesh: pipe: 8 (over y, core), expert: 16 (over x_hi, z), dp: 2 (over x_lo).
Axes of the slice: x: 4 (x_hi: 2, x_lo: 2; x = x_hi * 2 + x_lo), y: 4, z: 8, core: 2. Of those that a mesh axis runs over, the one named last changes fastest.
Arguments:
- fwd_in: bfloat16 [8, 4096, 3584], P('pipe', ('expert', 'dp')), may hold values from -6 to 6
- fwd_ids: int32 [8, 4096, 8], P('pipe', ('expert', 'dp')), may hold values from 0 to 255, all different within a row; in each aligned block of 128 rows (0 to 127, 128 to 255, ..., all dimensions but the last counted through in order) at most 8 rows name the same one
- fwd_score: float32 [8, 4096, 8], P('pipe', ('expert', 'dp')), may hold values from 0.05 to 1
- bwd_in: bfloat16 [8, 4096, 3584], P('pipe', ('expert', 'dp')), may hold values from -6 to 6
- bwd_ids: int32 [8, 4096, 8], P('pipe', ('expert', 'dp')), may hold values from 0 to 255, all different within a row; in each aligned block of 128 rows (0 to 127, 128 to 255, ..., all dimensions but the last counted through in order) at most 8 rows name the same one
- bwd_score: float32 [8, 4096, 8], P('pipe', ('expert', 'dp')), may hold values from 0.05 to 1
- bwd_cot: bfloat16 [8, 4096, 3584], P('pipe', ('expert', 'dp')), may hold values from -6 to 6
- w_gate: bfloat16 [8, 3584, 8192], P('pipe', None, ('expert', 'dp')), may hold values from -0.09375 to 0.09375
- w_up: bfloat16 [8, 3584, 8192], P('pipe', None, ('expert', 'dp')), may hold values from -0.09375 to 0.09375
- w_down: bfloat16 [8, 8192, 3584], P('pipe', ('expert', 'dp')), may hold values from -0.1875 to 0.1875
Outputs:
- fwd_out: bfloat16 [8, 4096, 3584], P('pipe', ('expert', 'dp'))
- bwd_out: bfloat16 [8, 4096, 3584], P('pipe', ('expert', 'dp'))
The draws below stay inside these ranges and needn't reach their ends.
Inputs may be any that keep to these rules, and one draw needn't show every extreme that they name: `fwd_ids`: each token names 8 different experts; in each aligned block of 128 rows of one section no expert is named by more than 8 rows. `bwd_ids`: each token names 8 different experts; in each aligned block of 128 rows of one section no expert is named by more than 8 rows.
All inputs are finite; a program needn't handle non-finite values.
Results may differ from the reference program's by a relative error of at most 0.0045.
Values may be sent and summed in bfloat16 or wider, within the bound.
No kernel may reach another device: no remote copies, remote signals or barrier semaphores. Data moves between devices by JAX's collectives and lax.ppermute only.
A program may use at most 64 MiB of HBM per device.

```python
import math
import jax
import jax.numpy as jnp
import numpy as np
from jax import lax

D = 3584
HID = 1024
ROUTED = 256
TOP = 8
TOK_DEV = 128
CAP = 8
EXPERTS = 8
SECTIONS = 8
TOKENS = 4096
N_EXPERT = 16
N_DP = 2


def block_levels(own_key, dims, split, smallest, high):
    def one(dim, shards_of):
        steps = jax.random.uniform(jax.random.fold_in(jax.random.fold_in(own_key, 6), dim), (shards_of,), jnp.float32, smallest / len(split), high / len(split))
        return jnp.repeat(jnp.exp(steps), dims[dim] // shards_of).reshape((-1,) + (1,) * (len(dims) - dim - 1))

    factor_of = one(*split[0])
    for cut in split[1:]:
        factor_of = factor_of * one(*cut)
    return factor_of


def routed_block(rng, own, number, rows, amount, top, reach, lean):
    sequence = jax.random.permutation(rng, amount)
    crowded, common = shares(amount, rows * top, reach, lean, True), shares(amount, rows * top, reach, lean, False)
    places = jnp.arange(amount)

    def named(lengths, offset_by):
        used = int((lengths > 0).sum())
        fixed = max(1, used // 4)
        moved = fixed + (places - fixed + offset_by * (used - fixed)) % max(1, amount - fixed)
        return jnp.zeros((amount,), jnp.int32).at[sequence[jnp.where(places < fixed, places, moved)]].set(jnp.asarray(lengths, jnp.int32))

    lengths = jnp.where(number % 4 == 0, named(crowded, number // 4), named(common, number - number // 4 - 1))
    mixed = jax.random.permutation(jax.random.fold_in(own, 3), amount)
    giver, receiver = mixed[0:amount // 2 * 2:2], mixed[1:amount // 2 * 2:2]
    slack = jnp.minimum(lengths[giver] - 1, reach - lengths[receiver]) // 2
    slack = jnp.where((giver == sequence[0]) | (receiver == sequence[0]) | (lengths[receiver] == 0), 0, jnp.maximum(slack, 0))
    moved = jax.random.randint(jax.random.fold_in(own, 4), (amount // 2,), 0, 1 << 20) % (slack + 1)
    lengths = lengths.at[giver].add(-moved).at[receiver].add(moved)
    labels = jnp.searchsorted(jnp.cumsum(lengths), jnp.arange(rows * top), side="right").astype(jnp.int32)
    table = labels.reshape(top, rows).T
    table = table[jax.random.permutation(jax.random.fold_in(own, 1), rows)]
    offset_by = jax.random.randint(jax.random.fold_in(own, 2), (rows, 1), 0, top)
    return jnp.take_along_axis(table, (jnp.arange(top)[None, :] + offset_by) % top, axis=1)


def shares(amount, total, bound, lean, full):
    loads = [(1 << 20) // math.isqrt(grade ** lean) + 1 for grade in range(1, amount + 1)]
    largest = bound if full else min(bound, max(-(-total // amount), total * loads[0] // sum(loads)))
    least = 1 if total - largest >= amount - 1 else 0
    given, rest = [largest] + [least] * (amount - 1), total - largest - least * (amount - 1)
    while rest > 0:
        candidates = [i for i in range(1, amount) if given[i] < largest] or [i for i in range(1, amount) if given[i] < bound]
        mass, remaining = sum([loads[i] for i in candidates]), rest
        for i in candidates:
            addition = min(bound - given[i], max(1, remaining * loads[i] // mass), rest)
            given[i] = given[i] + addition
            rest = rest - addition
    return np.array(given)


def bell_draw(own_key, dims, spread, bound, cuts=(), held_as=jnp.bfloat16):
    gain = block_levels(own_key, dims, cuts, -0.22, 0.18) if cuts else 1.0
    entries = jax.random.normal(own_key, dims, jnp.float32) * spread * gain
    return jnp.minimum(jnp.maximum(entries, -bound), bound).astype(held_as)


def setup_inputs(seed: int = 0) -> dict:
    keys = jax.random.split(jax.random.key(seed), 11)
    fwd_in = bell_draw(keys[0], (SECTIONS, TOKENS, D), 1.0, 6.0, ((0, 8), (1, 32)))
    fwd_ids_keys = jax.random.split(jax.random.fold_in(keys[1], 1), SECTIONS * TOKENS // TOK_DEV)
    fwd_ids_turns = jax.random.permutation(jax.random.fold_in(keys[1], 3), SECTIONS * TOKENS // TOK_DEV)
    fwd_ids = jax.vmap(lambda own, number: routed_block(jax.random.fold_in(keys[1], 2), own, number, TOK_DEV, ROUTED, TOP, CAP, 2))(fwd_ids_keys, fwd_ids_turns).reshape((SECTIONS, TOKENS, TOP))
    fwd_score = jnp.clip(0.05 + 0.95 * jax.random.uniform(keys[2], (SECTIONS, TOKENS, TOP), jnp.float32) ** block_levels(keys[2], (SECTIONS, TOKENS, TOP), ((0, 8), (1, 32)), -0.2, 0.2), 0.05, 1.0)
    bwd_in = bell_draw(keys[3], (SECTIONS, TOKENS, D), 1.0, 6.0, ((0, 8), (1, 32)))
    bwd_ids_keys = jax.random.split(jax.random.fold_in(keys[4], 1), SECTIONS * TOKENS // TOK_DEV)
    bwd_ids_turns = jax.random.permutation(jax.random.fold_in(keys[4], 3), SECTIONS * TOKENS // TOK_DEV)
    bwd_ids = jax.vmap(lambda own, number: routed_block(jax.random.fold_in(keys[4], 2), own, number, TOK_DEV, ROUTED, TOP, CAP, 2))(bwd_ids_keys, bwd_ids_turns).reshape((SECTIONS, TOKENS, TOP))
    bwd_score = jnp.clip(0.05 + 0.95 * jax.random.uniform(keys[5], (SECTIONS, TOKENS, TOP), jnp.float32) ** block_levels(keys[5], (SECTIONS, TOKENS, TOP), ((0, 8), (1, 32)), -0.2, 0.2), 0.05, 1.0)
    bwd_cot = bell_draw(keys[6], (SECTIONS, TOKENS, D), 1.0, 6.0, ((0, 8), (1, 32)))
    w_gate = bell_draw(keys[7], (SECTIONS, D, EXPERTS * HID), D ** -0.5, 0.09375, ((0, 8), (2, 32)))
    w_up = bell_draw(keys[8], (SECTIONS, D, EXPERTS * HID), D ** -0.5, 0.09375, ((0, 8), (2, 32)))
    w_down = bell_draw(keys[9], (SECTIONS, EXPERTS * HID, D), HID ** -0.5, 0.1875, ((0, 8), (1, 32)))
    return {"fwd_in": fwd_in, "fwd_ids": fwd_ids, "fwd_score": fwd_score, "bwd_in": bwd_in, "bwd_ids": bwd_ids, "bwd_score": bwd_score, "bwd_cot": bwd_cot, "w_gate": w_gate, "w_up": w_up, "w_down": w_down}


def expert_forward(rows, gate_w, up_w, down_w):
    gate_pre = jnp.dot(rows, gate_w, preferred_element_type=jnp.float32)
    up_pre = jnp.dot(rows, up_w, preferred_element_type=jnp.float32)
    hidden = (jax.nn.silu(gate_pre) * up_pre).astype(jnp.bfloat16)
    return jnp.dot(hidden, down_w, preferred_element_type=jnp.float32)


def expert_backward(rows, cotan, gate_w, up_w, down_w):
    gate_pre = jnp.dot(rows, gate_w, preferred_element_type=jnp.float32)
    up_pre = jnp.dot(rows, up_w, preferred_element_type=jnp.float32)
    grad_hidden = jnp.dot(cotan, down_w.T, preferred_element_type=jnp.float32)
    sigma = jax.nn.sigmoid(gate_pre)
    grad_gate = (grad_hidden * up_pre * sigma * (1.0 + gate_pre * (1.0 - sigma))).astype(jnp.bfloat16)
    grad_up = (grad_hidden * jax.nn.silu(gate_pre)).astype(jnp.bfloat16)
    return jnp.dot(grad_gate, gate_w.T, preferred_element_type=jnp.float32) + jnp.dot(grad_up, up_w.T, preferred_element_type=jnp.float32)


def apply_layer(tokens, ids, score, gate_cols, up_cols, down_rows, cotan, backward):
    mix = 2.5 * score / jnp.sum(score, axis=-1, keepdims=True)
    rows_total = N_EXPERT * N_DP * CAP
    gate_all = gate_cols.reshape(D, EXPERTS, HID).transpose(1, 0, 2)
    up_all = up_cols.reshape(D, EXPERTS, HID).transpose(1, 0, 2)
    down_all = down_rows.reshape(EXPERTS, HID, D)

    def one_expert(total, packed):
        index, gate_w, up_w, down_w = packed
        picked = ids == index
        weight = jnp.sum(jnp.where(picked, mix, 0.0), axis=-1)
        used = jnp.any(picked, axis=-1)
        count = jnp.sum(used.astype(jnp.int32))
        rows = jnp.nonzero(used, size=rows_total, fill_value=0)[0]
        valid = jnp.arange(rows_total, dtype=jnp.int32) < count
        factor = jnp.where(valid, weight[rows], 0.0)
        if backward:
            term = expert_backward(tokens[rows], cotan[rows], gate_w, up_w, down_w)
        else:
            term = expert_forward(tokens[rows], gate_w, up_w, down_w)
        term = lax.optimization_barrier(term.astype(jnp.bfloat16)).astype(jnp.float32)
        return total.at[rows].add(factor[:, None] * term), None

    start = jnp.zeros(tokens.shape, jnp.float32)
    indices = jnp.arange(EXPERTS, dtype=jnp.int32)
    total, unused = lax.scan(one_expert, start, (indices, gate_all, up_all, down_all))
    base = cotan if backward else tokens
    return (base.astype(jnp.float32) + total).astype(jnp.bfloat16)


def reference(fwd_in, fwd_ids, fwd_score, bwd_in, bwd_ids, bwd_score, bwd_cot, w_gate, w_up, w_down):
    def forward_section(packed):
        tokens, ids, score, gate_cols, up_cols, down_rows = packed
        return apply_layer(tokens, ids, score, gate_cols, up_cols, down_rows, None, False)

    def backward_section(packed):
        tokens, ids, score, cotan, gate_cols, up_cols, down_rows = packed
        return apply_layer(tokens, ids, score, gate_cols, up_cols, down_rows, cotan, True)

    fwd_done = lax.map(forward_section, (fwd_in, fwd_ids, fwd_score, w_gate, w_up, w_down))
    bwd_done = lax.map(backward_section, (bwd_in, bwd_ids, bwd_score, bwd_cot, w_gate, w_up, w_down))
    zeros = jnp.zeros(fwd_in[:1].shape, jnp.bfloat16)
    fwd_out = jnp.concatenate([zeros, fwd_done[:-1]], axis=0)
    bwd_out = jnp.concatenate([bwd_done[1:], zeros], axis=0)
    return fwd_out, bwd_out
```

```python
import jax
import jax.numpy as jnp
from jax import lax
from jax.experimental import pallas as pl
from jax.experimental.pallas import tpu as pltpu
from jax.sharding import PartitionSpec as P

CAP = 8
PAIRS = 4
BLOCK = 2 * CAP
HALF = PAIRS * CAP
HOME = PAIRS * BLOCK
BF16 = jnp.bfloat16
F32 = jnp.float32
CHUNKS = 2


def call(body, outs, args, flops=0, smem=()):
    total = sum(a.size * a.dtype.itemsize for a in args)
    total += sum(o.size * o.dtype.itemsize for o in outs)
    specs = [
        pl.BlockSpec(memory_space=pltpu.SMEM if i in smem else pltpu.VMEM)
        for i in range(len(args))
    ]
    return pl.pallas_call(
        body,
        out_shape=tuple(outs),
        in_specs=specs,
        out_specs=tuple(pl.BlockSpec(memory_space=pltpu.VMEM) for _ in outs),
        compiler_params=pltpu.CompilerParams(vmem_limit_bytes=48 * 1024 * 1024),
        cost_estimate=pl.CostEstimate(flops=flops, bytes_accessed=total, transcendentals=0),
    )(*args)


def shape(rows, cols, dtype=BF16):
    return jax.ShapeDtypeStruct((rows, cols), dtype)


def dot(a, b):
    return lax.dot_general(a, b, (((1,), (0,)), ((), ())), preferred_element_type=F32)


def dot_t(a, b):
    return lax.dot_general(a, b, (((1,), (1,)), ((), ())), preferred_element_type=F32)


def section_perm(move):
    pairs = []
    for xh in range(2):
        for z in range(8):
            for d in range(2):
                nxh, nz, nd = move(xh, z, d)
                pairs.append(((xh * 8 + z) * 2 + d, (nxh * 8 + nz % 8) * 2 + nd))
    return pairs


def inverse(pairs):
    return [(b, a) for a, b in pairs]


ACROSS_XHI = section_perm(lambda xh, z, d: (1 - xh, z, 1 - d))
SHIFT_A = section_perm(lambda xh, z, d: (xh, z + (2 if z % 2 == 0 else -2), d))
SHIFT_B = section_perm(lambda xh, z, d: (xh, z + (-1 if z % 2 == 0 else 1), d))
SHIFT_C = section_perm(lambda xh, z, d: (xh, z + (-3 if z % 2 == 0 else 3), d))
Z_PAIR = section_perm(lambda xh, z, d: (xh, z ^ 1, d))
DP_PAIR = section_perm(lambda xh, z, d: (xh, z, 1 - d))
STAY = section_perm(lambda xh, z, d: (xh, z, d))


def move(value, pairs):
    return lax.ppermute(value, ("expert", "dp"), pairs)


def relay(value, pairs, step):
    sections = lax.axis_size("pipe")
    size = len(pairs)
    full = []
    for s in range(sections):
        t = s + step
        if 0 <= t < sections:
            full += [(s * size + a, t * size + b) for a, b in pairs]
    return lax.ppermute(value, ("pipe", "expert", "dp"), full)


def slot_tables(where_ref, ids_ref, score_ref):
    tokens = ids_ref.shape[0]
    where = where_ref[0]
    xh = where // 8
    z = where % 8
    pair = z // 2
    sign = 1 - 2 * (z % 2)
    shape2 = (tokens, 2 * HOME)
    lane = lax.broadcasted_iota(jnp.int32, shape2, 1)
    slot = lane & (HOME - 1)
    half = slot >> 5
    q = (slot >> 3) & 3
    rank_of = slot & 7
    gray = q ^ (q >> 1)
    expert = (xh ^ half) * PAIRS + ((pair + sign * gray) & 3)
    ids = ids_ref[...]
    score = score_ref[...]
    mix = 2.5 * score / jnp.sum(score, axis=1, keepdims=True)
    hit = jnp.zeros(shape2, F32)
    weight = jnp.zeros(shape2, F32)
    for k in range(ids.shape[1]):
        same = ids[:, k : k + 1] == expert
        hit = jnp.where(same, 1.0, hit)
        weight = jnp.where(same, mix[:, k : k + 1], weight)
    row = lax.broadcasted_iota(jnp.int32, (tokens, tokens), 0)
    col = lax.broadcasted_iota(jnp.int32, (tokens, tokens), 1)
    before = jnp.where(row > col, 1.0, 0.0).astype(BF16)
    rank = dot(before, hit.astype(BF16))
    taken = jnp.where((hit > 0.0) & (rank == rank_of.astype(F32)), 1.0, 0.0)
    weight = weight * taken
    high = weight.astype(BF16).astype(F32)
    comb = jnp.where(lane < HOME, high, weight - high).astype(BF16)
    dispatch = jnp.transpose(taken)[:HOME].astype(BF16)
    return dispatch, comb


def pack_one(where_ref, ids_ref, score_ref, tok_ref, own_ref, far_ref, comb_ref):
    dispatch, comb = slot_tables(where_ref, ids_ref, score_ref)
    comb_ref[...] = comb
    own_ref[...] = dot(dispatch[:HALF], tok_ref[...]).astype(BF16)
    far_ref[...] = dot(dispatch[HALF:], tok_ref[...]).astype(BF16)


def pack_two(
    where_ref, ids_ref, score_ref, tok_ref, cot_ref,
    own_ref, far_ref, cown_ref, cfar_ref, comb_ref,
):
    dispatch, comb = slot_tables(where_ref, ids_ref, score_ref)
    comb_ref[...] = comb
    own_ref[...] = dot(dispatch[:HALF], tok_ref[...]).astype(BF16)
    far_ref[...] = dot(dispatch[HALF:], tok_ref[...]).astype(BF16)
    cown_ref[...] = dot(dispatch[:HALF], cot_ref[...]).astype(BF16)
    cfar_ref[...] = dot(dispatch[HALF:], cot_ref[...]).astype(BF16)


def weave_body(own_ref, got_ref, *block_refs):
    own = own_ref[...].astype(F32)
    got = got_ref[...].astype(F32)
    for q, ref in enumerate(block_refs):
        rows = slice(q * CAP, (q + 1) * CAP)
        ref[...] = jnp.concatenate([own[rows], got[rows]], axis=0).astype(BF16)


def part_body(b0, b1, b2, b3, own_ref, far_ref):
    blocks = [b[...].astype(F32) for b in (b0, b1, b2, b3)]
    own_ref[...] = jnp.concatenate([b[:CAP] for b in blocks], axis=0).astype(BF16)
    far_ref[...] = jnp.concatenate([b[CAP:] for b in blocks], axis=0).astype(BF16)


def hidden_body(a_ref, b_ref, wg_ref, wu_ref, out_ref):
    rows = jnp.concatenate([a_ref[...], b_ref[...]], axis=0)
    gate = dot(rows, wg_ref[...])
    up = dot(rows, wu_ref[...])
    out_ref[...] = (gate * jax.nn.sigmoid(gate) * up).astype(BF16)


def down_body(mine_ref, theirs_ref, wd_ref, wdp_ref, keep_ref, send_ref):
    total = dot(mine_ref[...], wd_ref[...]) + dot(theirs_ref[...], wdp_ref[...])
    keep_ref[...] = total[:HOME]
    send_ref[...] = total[HOME:].astype(BF16)


def finish_body(keep_ref, got_ref, *block_refs):
    total = keep_ref[...] + got_ref[...].astype(F32)
    for q, ref in enumerate(block_refs):
        ref[...] = total[q * BLOCK : (q + 1) * BLOCK].astype(BF16)


def slopes(rows, wg_ref, wu_ref):
    gate = dot(rows, wg_ref[...])
    up = dot(rows, wu_ref[...])
    sigma = jax.nn.sigmoid(gate)
    return up * sigma * (1.0 + gate * (1.0 - sigma)), gate * sigma


def slope_body(a_ref, b_ref, wg_ref, wu_ref, sg_ref, su_ref):
    rows = jnp.concatenate([a_ref[...], b_ref[...]], axis=0)
    sg, su = slopes(rows, wg_ref, wu_ref)
    sg_ref[...] = sg
    su_ref[...] = su


def grad_hidden_body(a_ref, b_ref, wd_ref, wdp_ref, mine_ref, send_ref):
    rows = jnp.concatenate([a_ref[...], b_ref[...]], axis=0)
    mine_ref[...] = dot_t(rows, wd_ref[...])
    send_ref[...] = dot_t(rows, wdp_ref[...])


def grads_body(
    a_ref, b_ref, wg_ref, wu_ref, sg_ref, su_ref, mine_ref, got_ref, gg_ref, gu_ref
):
    rows = jnp.concatenate([a_ref[...], b_ref[...]], axis=0)
    count = rows.shape[0]
    sgx, sux = slopes(rows, wg_ref, wu_ref)
    mine = mine_ref[...]
    got = got_ref[...]
    gg_ref[:count] = (mine * sg_ref[...]).astype(BF16)
    gg_ref[count:] = (got * sgx).astype(BF16)
    gu_ref[:count] = (mine * su_ref[...]).astype(BF16)
    gu_ref[count:] = (got * sux).astype(BF16)


def back_body(gg_ref, gu_ref, wg_ref, wu_ref, keep_ref, send_ref):
    total = dot_t(gg_ref[...], wg_ref[...]) + dot_t(gu_ref[...], wu_ref[...])
    count = keep_ref.shape[0]
    keep_ref[...] = total[:count]
    send_ref[...] = total[count:].astype(BF16)


def fold_body(keep_ref, got_ref, own_ref, send_ref):
    total = keep_ref[...] + got_ref[...].astype(F32)
    own_ref[...] = total[:HOME]
    send_ref[...] = total[HOME:].astype(BF16)


def combine_body(base_ref, comb_ref, *rest):
    out_ref = rest[-1]
    comb = comb_ref[...]
    col = 0
    for i in range(0, len(rest) - 1, 2):
        rows = jnp.concatenate([rest[i][...], rest[i + 1][...]], axis=0)
        width = rows.shape[1]
        cols = slice(col, col + width)
        total = dot(comb, jnp.concatenate([rows, rows], axis=0))
        out_ref[:, cols] = (base_ref[:, cols].astype(F32) + total).astype(BF16)
        col += width


def back_call(gg, gu, wg, wu, index, chunks):
    width = wg.shape[0] // chunks
    rows = gg.shape[0]
    whole = pl.BlockSpec((rows, gg.shape[1]), lambda i: (0, 0))
    part = pl.BlockSpec((width, wg.shape[1]), lambda i: (index, 0))
    half = rows // 2
    return pl.pallas_call(
        back_body,
        grid=(1,),
        out_shape=(shape(half, width, F32), shape(half, width)),
        in_specs=[whole, whole, part, part],
        out_specs=(
            pl.BlockSpec((half, width), lambda i: (0, 0)),
            pl.BlockSpec((half, width), lambda i: (0, 0)),
        ),
        compiler_params=pltpu.CompilerParams(vmem_limit_bytes=48 * 1024 * 1024),
        cost_estimate=pl.CostEstimate(
            flops=4 * rows * width * gg.shape[1],
            bytes_accessed=4 * width * wg.shape[1] + 6 * half * width,
            transcendentals=0,
        ),
    )(gg, gu, wg, wu)


def gather_home(own, far):
    width = own.shape[1]
    got = move(far, ACROSS_XHI)
    blocks = call(weave_body, [shape(BLOCK, width)] * PAIRS, [own, got])
    home = jnp.concatenate(
        [
            blocks[0],
            move(blocks[1], SHIFT_A),
            move(blocks[2], SHIFT_B),
            move(blocks[3], SHIFT_C),
        ],
        axis=0,
    )
    return home, move(home, Z_PAIR)


def send_back(blocks, step):
    width = blocks[0].shape[1]
    b0 = blocks[0]
    b1 = move(blocks[1], inverse(SHIFT_A))
    b2 = move(blocks[2], inverse(SHIFT_B))
    b3 = move(blocks[3], inverse(SHIFT_C))
    own, far = call(part_body, [shape(HALF, width)] * 2, [b0, b1, b2, b3])
    return relay(own, STAY, step), relay(far, ACROSS_XHI, step)


def per_device(
    fwd_in, fwd_ids, fwd_score, bwd_in, bwd_ids, bwd_score, bwd_cot, w_gate, w_up, w_down
):
    tokens, width = fwd_in.shape[1:]
    wg, wu, wd = w_gate[0], w_up[0], w_down[0]
    hid = wg.shape[1]
    wdp = move(wd, DP_PAIR)
    where = lax.axis_index("expert").astype(jnp.int32).reshape(1)
    packed = [shape(HALF, width)] * 2
    table = [shape(tokens, 2 * HOME)]

    own, far, fcomb = call(
        pack_one, packed + table, [where, fwd_ids[0], fwd_score[0], fwd_in[0]], smem=(0,)
    )
    fy, fyz = gather_home(own, far)
    bown, bfar, cown, cfar, bcomb = call(
        pack_two,
        packed * 2 + table,
        [where, bwd_ids[0], bwd_score[0], bwd_in[0], bwd_cot[0]],
        smem=(0,),
    )
    by, byz = gather_home(bown, bfar)
    cy, cyz = gather_home(cown, cfar)
    fyx, fyzx = move(fy, DP_PAIR), move(fyz, DP_PAIR)
    byx, byzx = move(by, DP_PAIR), move(byz, DP_PAIR)

    fbase = relay(fwd_in[0], STAY, 1)
    fcomb = relay(fcomb, STAY, 1)
    bbase = relay(bwd_cot[0], STAY, -1)
    bcomb = relay(bcomb, STAY, -1)

    rows = 2 * HOME
    proj = 4 * rows * width * hid
    (mine,) = call(hidden_body, [shape(rows, hid)], [fy, fyz, wg, wu], proj)
    (theirs,) = call(hidden_body, [shape(rows, hid)], [fyx, fyzx, wg, wu], proj)
    theirs = move(theirs, DP_PAIR)
    keep, send = call(
        down_body, [shape(HOME, width, F32), shape(HOME, width)], [mine, theirs, wd, wdp], proj
    )
    blocks = call(finish_body, [shape(BLOCK, width)] * PAIRS, [keep, move(send, Z_PAIR)])
    fown, ffar = send_back(blocks, 1)
    (fwd_out,) = call(combine_body, [shape(tokens, width)], [fbase, fcomb, fown, ffar])

    sg, su = call(slope_body, [shape(rows, hid, F32)] * 2, [by, byz, wg, wu], proj)
    gh, gh_send = call(
        grad_hidden_body, [shape(rows, hid, F32)] * 2, [cy, cyz, wd, wdp], proj
    )
    gh_got = move(gh_send, DP_PAIR)
    gg, gu = call(
        grads_body,
        [shape(2 * rows, hid)] * 2,
        [byx, byzx, wg, wu, sg, su, gh, gh_got],
        proj,
    )
    pieces = []
    for index in range(CHUNKS):
        part = width // CHUNKS
        keep, send = back_call(gg, gu, wg, wu, index, CHUNKS)
        keep, send = call(
            fold_body,
            [shape(HOME, part, F32), shape(HOME, part)],
            [keep, move(send, DP_PAIR)],
        )
        blocks = call(finish_body, [shape(BLOCK, part)] * PAIRS, [keep, move(send, Z_PAIR)])
        pieces += send_back(blocks, -1)
    (bwd_out,) = call(combine_body, [shape(tokens, width)], [bbase, bcomb] + pieces)
    return fwd_out[None], bwd_out[None]


def solution(mesh):
    rows = P("pipe", ("expert", "dp"), None)
    cols = P("pipe", None, ("expert", "dp"))
    return jax.shard_map(
        per_device,
        mesh=mesh,
        in_specs=(rows,) * 7 + (cols, cols, rows),
        out_specs=(rows, rows),
        check_vma=False,
    )
```

```python
import jax
import jax.numpy as jnp
from jax import lax
from jax.experimental import pallas as pl
from jax.experimental.pallas import tpu as pltpu
from jax.sharding import PartitionSpec as P

CAP = 8
PAIRS = 4
BLOCK = 2 * CAP
HALF = PAIRS * CAP
HOME = PAIRS * BLOCK
BF16 = jnp.bfloat16
F32 = jnp.float32


def call(body, outs, args, flops=0, smem=(), after=(), limit=48):
    total = sum(a.size * a.dtype.itemsize for a in args)
    total += sum(o.size * o.dtype.itemsize for o in outs)
    specs = [
        pl.BlockSpec(memory_space=pltpu.SMEM if i in smem else pltpu.VMEM)
        for i in range(len(args))
    ]
    specs += [pl.BlockSpec(memory_space=pl.ANY)] * len(after)
    used, extra = len(args), len(after)

    def run(*refs):
        body(*refs[:used], *refs[used + extra :])

    return pl.pallas_call(
        run,
        out_shape=tuple(outs),
        in_specs=specs,
        out_specs=tuple(pl.BlockSpec(memory_space=pltpu.VMEM) for _ in outs),
        compiler_params=pltpu.CompilerParams(vmem_limit_bytes=limit * 1024 * 1024),
        cost_estimate=pl.CostEstimate(flops=flops, bytes_accessed=total, transcendentals=0),
    )(*args, *after)


def shape(rows, cols, dtype=BF16):
    return jax.ShapeDtypeStruct((rows, cols), dtype)


def dot(a, b):
    return lax.dot_general(a, b, (((1,), (0,)), ((), ())), preferred_element_type=F32)


def dot_t(a, b):
    return lax.dot_general(a, b, (((1,), (1,)), ((), ())), preferred_element_type=F32)


def section_perm(move):
    pairs = []
    for xh in range(2):
        for z in range(8):
            for d in range(2):
                nxh, nz, nd = move(xh, z, d)
                pairs.append(((xh * 8 + z) * 2 + d, (nxh * 8 + nz % 8) * 2 + nd))
    return pairs


def inverse(pairs):
    return [(b, a) for a, b in pairs]


ACROSS_XHI = section_perm(lambda xh, z, d: (1 - xh, z, 1 - d))
SHIFT_A = section_perm(lambda xh, z, d: (xh, z + (2 if z % 2 == 0 else -2), d))
SHIFT_B = section_perm(lambda xh, z, d: (xh, z + (-1 if z % 2 == 0 else 1), d))
SHIFT_C = section_perm(lambda xh, z, d: (xh, z + (-3 if z % 2 == 0 else 3), d))
Z_PAIR = section_perm(lambda xh, z, d: (xh, z ^ 1, d))
DP_PAIR = section_perm(lambda xh, z, d: (xh, z, 1 - d))
STAY = section_perm(lambda xh, z, d: (xh, z, d))


def move(value, pairs):
    return lax.ppermute(value, ("expert", "dp"), pairs)


def relay(value, pairs, step):
    sections = lax.axis_size("pipe")
    size = len(pairs)
    full = []
    for s in range(sections):
        t = s + step
        if 0 <= t < sections:
            full += [(s * size + a, t * size + b) for a, b in pairs]
    return lax.ppermute(value, ("pipe", "expert", "dp"), full)


def slot_tables(where_ref, ids_ref, score_ref):
    choices, tokens = ids_ref.shape
    where = where_ref[0]
    xh = where // 8
    z = where % 8
    pair = z // 2
    sign = 1 - 2 * (z % 2)
    shape2 = (2 * HOME, tokens)
    index = lax.broadcasted_iota(jnp.int32, shape2, 0)
    slot = index & (HOME - 1)
    half = slot >> 5
    q = (slot >> 3) & 3
    rank_of = slot & 7
    gray = q ^ (q >> 1)
    expert = (xh ^ half) * PAIRS + ((pair + sign * gray) & 3)
    ids = ids_ref[...]
    score = score_ref[...]
    mix = 2.5 * score / jnp.sum(score, axis=0, keepdims=True)
    hit = jnp.zeros(shape2, F32)
    weight = jnp.zeros(shape2, F32)
    for k in range(choices):
        same = ids[k : k + 1] == expert
        hit = jnp.where(same, 1.0, hit)
        weight = jnp.where(same, mix[k : k + 1], weight)
    row = lax.broadcasted_iota(jnp.int32, (tokens, tokens), 0)
    col = lax.broadcasted_iota(jnp.int32, (tokens, tokens), 1)
    before = jnp.where(row < col, 1.0, 0.0).astype(BF16)
    rank = dot(hit.astype(BF16), before)
    taken = jnp.where((hit > 0.0) & (rank == rank_of.astype(F32)), 1.0, 0.0)
    weight = weight * taken
    high = weight.astype(BF16).astype(F32)
    comb = jnp.where(index < HOME, high, weight - high)
    return taken[:HOME].astype(BF16), jnp.transpose(comb).astype(BF16)


def pack_body(where_ref, ids_ref, score_ref, *refs):
    tok_refs, (own_ref, far_ref, comb_ref) = refs[:-3], refs[-3:]
    dispatch, comb = slot_tables(where_ref, ids_ref, score_ref)
    comb_ref[...] = comb
    for i, ref in enumerate(tok_refs):
        rows = slice(i * HALF, (i + 1) * HALF)
        picked = dot(dispatch, ref[...]).astype(BF16)
        own_ref[rows] = picked[:HALF]
        far_ref[rows] = picked[HALF:]


def weave_body(own_ref, got_ref, *block_refs):
    own = own_ref[...].astype(F32)
    got = got_ref[...].astype(F32)
    for q, ref in enumerate(block_refs):
        parts = []
        for base in range(0, own.shape[0], HALF):
            rows = slice(base + q * CAP, base + (q + 1) * CAP)
            parts += [own[rows], got[rows]]
        ref[...] = jnp.concatenate(parts, axis=0).astype(BF16)


def part_body(b0, b1, b2, b3, own_ref, far_ref):
    blocks = [b[...].astype(F32) for b in (b0, b1, b2, b3)]
    own_ref[...] = jnp.concatenate([b[:CAP] for b in blocks], axis=0).astype(BF16)
    far_ref[...] = jnp.concatenate([b[CAP:] for b in blocks], axis=0).astype(BF16)


def join_body(*refs):
    refs[-1][...] = jnp.concatenate([r[...] for r in refs[:-1]], axis=0)


def hidden_body(rows_ref, wg_ref, wu_ref, out_ref):
    rows = rows_ref[...]
    gate = dot(rows, wg_ref[...])
    up = dot(rows, wu_ref[...])
    out_ref[...] = (gate * jax.nn.sigmoid(gate) * up).astype(BF16)


def down_body(mine_ref, theirs_ref, wd_ref, wdp_ref, keep_ref, send_ref):
    total = dot(mine_ref[...], wd_ref[...]) + dot(theirs_ref[...], wdp_ref[...])
    keep_ref[...] = total[:HOME]
    send_ref[...] = total[HOME:].astype(BF16)


def finish_body(*refs):
    blocks, pairs = refs[-PAIRS:], refs[:-PAIRS]
    col = 0
    for i in range(0, len(pairs), 2):
        total = pairs[i][...] + pairs[i + 1][...].astype(F32)
        cols = slice(col, col + total.shape[1])
        for q, ref in enumerate(blocks):
            ref[:, cols] = total[q * BLOCK : (q + 1) * BLOCK].astype(BF16)
        col += total.shape[1]


def slopes(rows, wg_ref, wu_ref):
    gate = dot(rows, wg_ref[...])
    up = dot(rows, wu_ref[...])
    sigma = jax.nn.sigmoid(gate)
    return up * sigma * (1.0 + gate * (1.0 - sigma)), gate * sigma


def slope_body(rows_ref, wg_ref, wu_ref, sg_ref, su_ref):
    sg_ref[...], su_ref[...] = slopes(rows_ref[...], wg_ref, wu_ref)


def grad_hidden_body(rows_ref, wd_ref, wdp_ref, mine_ref, send_ref):
    rows = rows_ref[...]
    mine_ref[...] = dot_t(rows, wd_ref[...])
    send_ref[...] = dot_t(rows, wdp_ref[...])


def grads_body(
    rows_ref, wg_ref, wu_ref, sg_ref, su_ref, mine_ref, got_ref, gg_ref, gu_ref
):
    rows = rows_ref[...]
    count = rows.shape[0]
    sgx, sux = slopes(rows, wg_ref, wu_ref)
    mine = mine_ref[...]
    got = got_ref[...]
    gg_ref[:count] = (mine * sg_ref[...]).astype(BF16)
    gg_ref[count:] = (got * sgx).astype(BF16)
    gu_ref[:count] = (mine * su_ref[...]).astype(BF16)
    gu_ref[count:] = (got * sux).astype(BF16)


def back_x_body(gg_ref, gu_ref, wg_ref, wu_ref, keep_ref, send_ref):
    total = dot_t(gg_ref[...], wg_ref[...]) + dot_t(gu_ref[...], wu_ref[...])
    count = keep_ref.shape[0]
    keep_ref[...] = total[:count]
    send_ref[...] = total[count:].astype(BF16)


def back_z_body(gg_ref, gu_ref, wg_ref, wu_ref, keep_ref, send_ref):
    total = dot_t(gg_ref[...], wg_ref[...]) + dot_t(gu_ref[...], wu_ref[...])
    keep_ref[:HOME] = total[:HOME]
    keep_ref[HOME:] = total[2 * HOME : 3 * HOME]
    send_ref[:HOME] = total[HOME : 2 * HOME].astype(BF16)
    send_ref[HOME:] = total[3 * HOME :].astype(BF16)


def fold_body(keep_ref, got_ref, own_ref, send_ref):
    total = keep_ref[...] + got_ref[...].astype(F32)
    own_ref[...] = total[:HOME]
    send_ref[...] = total[HOME:].astype(BF16)


def combine_body(base_ref, comb_ref, own_ref, far_ref, out_ref):
    rows = jnp.concatenate([own_ref[...], far_ref[...]], axis=0)
    total = dot(comb_ref[...], jnp.concatenate([rows, rows], axis=0))
    out_ref[...] = (base_ref[...].astype(F32) + total).astype(BF16)


def back_call(body, gg, gu, wg, wu, index, chunks):
    width = wg.shape[0] // chunks
    rows = gg.shape[0]
    whole = pl.BlockSpec((rows, gg.shape[1]), lambda i: (0, 0))
    part = pl.BlockSpec((width, wg.shape[1]), lambda i: (index, 0))
    half = rows // 2
    return pl.pallas_call(
        body,
        grid=(1,),
        out_shape=(shape(half, width, F32), shape(half, width)),
        in_specs=[whole, whole, part, part],
        out_specs=(
            pl.BlockSpec((half, width), lambda i: (0, 0)),
            pl.BlockSpec((half, width), lambda i: (0, 0)),
        ),
        compiler_params=pltpu.CompilerParams(vmem_limit_bytes=48 * 1024 * 1024),
        cost_estimate=pl.CostEstimate(
            flops=4 * rows * width * gg.shape[1],
            bytes_accessed=4 * width * wg.shape[1] + 6 * half * width,
            transcendentals=0,
        ),
    )(gg, gu, wg, wu)


def join(parts, after=()):
    rows = sum(p.shape[0] for p in parts)
    return call(join_body, [shape(rows, parts[0].shape[1])], parts, after=after)[0]


def shifts(blocks, back):
    a, b, c = SHIFT_A, SHIFT_B, SHIFT_C
    if back:
        a, b, c = inverse(a), inverse(b), inverse(c)
    return [blocks[0], move(blocks[1], a), move(blocks[2], b), move(blocks[3], c)]


def per_device(
    fwd_in, fwd_ids, fwd_score, bwd_in, bwd_ids, bwd_score, bwd_cot, w_gate, w_up, w_down
):
    tokens, width = fwd_in.shape[1:]
    wg, wu, wd = w_gate[0], w_up[0], w_down[0]
    hid = wg.shape[1]
    rows = 2 * HOME
    proj = 4 * rows * width * hid
    wdp = move(wd, DP_PAIR)
    where = lax.axis_index("expert").astype(jnp.int32).reshape(1)
    table = shape(tokens, 2 * HOME)

    own, far, fcomb = call(
        pack_body,
        [shape(HALF, width)] * 2 + [table],
        [where, fwd_ids[0].T, fwd_score[0].T, fwd_in[0]],
        smem=(0,),
        limit=60,
    )
    bown, bfar, bcomb = call(
        pack_body,
        [shape(2 * HALF, width)] * 2 + [table],
        [where, bwd_ids[0].T, bwd_score[0].T, bwd_in[0], bwd_cot[0]],
        smem=(0,),
        limit=60,
        after=(far,),
    )
    bbase = relay(bwd_cot[0], STAY, -1)
    bcomb = relay(bcomb, STAY, -1)
    blocks = call(weave_body, [shape(BLOCK, width)] * PAIRS, [own, move(far, ACROSS_XHI)])
    fy = jnp.concatenate(shifts(blocks, False), axis=0)
    bblocks = call(
        weave_body,
        [shape(2 * BLOCK, width)] * PAIRS,
        [bown, move(bfar, ACROSS_XHI)],
        after=(fy, bcomb),
    )
    fy = jnp.concatenate([fy, move(fy, Z_PAIR)], axis=0)
    fyx = move(fy, DP_PAIR)
    (mine,) = call(hidden_body, [shape(rows, hid)], [fy, wg, wu], proj)

    parts = shifts(bblocks, False)
    by = jnp.concatenate([p[:BLOCK] for p in parts], axis=0)
    cy = jnp.concatenate([p[BLOCK:] for p in parts], axis=0)
    byz = move(by, Z_PAIR)
    cy = jnp.concatenate([cy, move(cy, Z_PAIR)], axis=0)

    (theirs,) = call(hidden_body, [shape(rows, hid)], [fyx, wg, wu], proj, after=(mine,))
    theirs = move(theirs, DP_PAIR)
    by = join([by, byz], after=(theirs,))
    byx = move(by, DP_PAIR)
    keep, send = call(
        down_body, [shape(HOME, width, F32), shape(HOME, width)], [mine, theirs, wd, wdp], proj
    )
    blocks = call(finish_body, [shape(BLOCK, width)] * PAIRS, [keep, move(send, Z_PAIR)])
    own, far = call(part_body, [shape(HALF, width)] * 2, shifts(blocks, True))
    far = move(far, ACROSS_XHI)
    (fwd_out,) = call(combine_body, [shape(tokens, width)], [fwd_in[0], fcomb, own, far])
    fwd_out = relay(fwd_out, STAY, 1)

    sg, su = call(
        slope_body, [shape(rows, hid, F32)] * 2, [by, wg, wu], proj, after=(bbase,)
    )
    gh, gh_send = call(grad_hidden_body, [shape(rows, hid, F32)] * 2, [cy, wd, wdp], proj)
    gh_got = move(gh_send, DP_PAIR)
    gg, gu = call(
        grads_body, [shape(2 * rows, hid)] * 2, [byx, wg, wu, sg, su, gh, gh_got], proj
    )
    half = width // 2
    fold = [shape(HOME, half, F32), shape(HOME, half)]
    xkeep, xsend = back_call(back_x_body, gg, gu, wg, wu, 0, 2)
    zkeep, zsend = back_call(back_z_body, gg, gu, wg, wu, 1, 2)
    xgot, zgot = move(xsend, DP_PAIR), move(zsend, Z_PAIR)
    xkeep, xsend = call(fold_body, fold, [xkeep, xgot])
    zkeep, zsend = call(fold_body, fold, [zkeep, zgot])
    xgot, zgot = move(xsend, Z_PAIR), move(zsend, DP_PAIR)
    blocks = call(
        finish_body, [shape(BLOCK, width)] * PAIRS, [xkeep, xgot, zkeep, zgot]
    )
    own, far = call(part_body, [shape(HALF, width)] * 2, shifts(blocks, True))
    own, far = relay(own, STAY, -1), relay(far, ACROSS_XHI, -1)
    (bwd_out,) = call(combine_body, [shape(tokens, width)], [bbase, bcomb, own, far])
    return fwd_out[None], bwd_out[None]


def solution(mesh):
    rows = P("pipe", ("expert", "dp"), None)
    cols = P("pipe", None, ("expert", "dp"))
    return jax.shard_map(
        per_device,
        mesh=mesh,
        in_specs=(rows,) * 7 + (cols, cols, rows),
        out_specs=(rows, rows),
        check_vma=False,
    )
```

```python
import jax
import jax.numpy as jnp
from jax import lax
from jax.experimental import pallas as pl
from jax.experimental.pallas import tpu as pltpu
from jax.sharding import PartitionSpec as P

CAP = 8
PAIRS = 4
BLOCK = 2 * CAP
HALF = PAIRS * CAP
HOME = PAIRS * BLOCK
BF16 = jnp.bfloat16
F32 = jnp.float32


def call(body, outs, args, flops=0, smem=(), after=(), limit=48):
    total = sum(a.size * a.dtype.itemsize for a in args)
    total += sum(o.size * o.dtype.itemsize for o in outs)
    specs = [
        pl.BlockSpec(memory_space=pltpu.SMEM if i in smem else pltpu.VMEM)
        for i in range(len(args))
    ]
    specs += [pl.BlockSpec(memory_space=pl.ANY)] * len(after)
    used, extra = len(args), len(after)

    def run(*refs):
        body(*refs[:used], *refs[used + extra :])

    return pl.pallas_call(
        run,
        out_shape=tuple(outs),
        in_specs=specs,
        out_specs=tuple(pl.BlockSpec(memory_space=pltpu.VMEM) for _ in outs),
        compiler_params=pltpu.CompilerParams(vmem_limit_bytes=limit * 1024 * 1024),
        cost_estimate=pl.CostEstimate(flops=flops, bytes_accessed=total, transcendentals=0),
    )(*args, *after)


def shape(rows, cols, dtype=BF16):
    return jax.ShapeDtypeStruct((rows, cols), dtype)


def dot(a, b):
    return lax.dot_general(a, b, (((1,), (0,)), ((), ())), preferred_element_type=F32)


def dot_t(a, b):
    return lax.dot_general(a, b, (((1,), (1,)), ((), ())), preferred_element_type=F32)


def section_perm(move):
    pairs = []
    for xh in range(2):
        for z in range(8):
            for d in range(2):
                nxh, nz, nd = move(xh, z, d)
                pairs.append(((xh * 8 + z) * 2 + d, (nxh * 8 + nz % 8) * 2 + nd))
    return pairs


def inverse(pairs):
    return [(b, a) for a, b in pairs]


ACROSS_XHI = section_perm(lambda xh, z, d: (1 - xh, z, 1 - d))
SHIFT_A = section_perm(lambda xh, z, d: (xh, z + (2 if z % 2 == 0 else -2), d))
SHIFT_B = section_perm(lambda xh, z, d: (xh, z + (-1 if z % 2 == 0 else 1), d))
SHIFT_C = section_perm(lambda xh, z, d: (xh, z + (-3 if z % 2 == 0 else 3), d))
Z_PAIR = section_perm(lambda xh, z, d: (xh, z ^ 1, d))
DP_PAIR = section_perm(lambda xh, z, d: (xh, z, 1 - d))
STAY = section_perm(lambda xh, z, d: (xh, z, d))


def move(value, pairs):
    return lax.ppermute(value, ("expert", "dp"), pairs)


def relay(value, pairs, step):
    sections = lax.axis_size("pipe")
    size = len(pairs)
    full = []
    for s in range(sections):
        t = s + step
        if 0 <= t < sections:
            full += [(s * size + a, t * size + b) for a, b in pairs]
    return lax.ppermute(value, ("pipe", "expert", "dp"), full)


def slot_tables(where_ref, ids_ref, score_ref):
    choices, tokens = ids_ref.shape
    where = where_ref[0]
    xh = where // 8
    z = where % 8
    pair = z // 2
    sign = 1 - 2 * (z % 2)
    shape2 = (2 * HOME, tokens)
    index = lax.broadcasted_iota(jnp.int32, shape2, 0)
    slot = index & (HOME - 1)
    half = slot >> 5
    q = (slot >> 3) & 3
    rank_of = slot & 7
    gray = q ^ (q >> 1)
    expert = (xh ^ half) * PAIRS + ((pair + sign * gray) & 3)
    ids = ids_ref[...]
    score = score_ref[...]
    mix = 2.5 * score / jnp.sum(score, axis=0, keepdims=True)
    hit = jnp.zeros(shape2, F32)
    weight = jnp.zeros(shape2, F32)
    for k in range(choices):
        same = ids[k : k + 1] == expert
        hit = jnp.where(same, 1.0, hit)
        weight = jnp.where(same, mix[k : k + 1], weight)
    row = lax.broadcasted_iota(jnp.int32, (tokens, tokens), 0)
    col = lax.broadcasted_iota(jnp.int32, (tokens, tokens), 1)
    before = jnp.where(row < col, 1.0, 0.0).astype(BF16)
    rank = dot(hit.astype(BF16), before)
    taken = jnp.where((hit > 0.0) & (rank == rank_of.astype(F32)), 1.0, 0.0)
    weight = weight * taken
    high = weight.astype(BF16).astype(F32)
    comb = jnp.where(index < HOME, high, weight - high)
    return taken[:HOME].astype(BF16), jnp.transpose(comb).astype(BF16)


def pack_body(where_ref, ids_ref, score_ref, *refs):
    tok_refs, (own_ref, far_ref, comb_ref) = refs[:-3], refs[-3:]
    dispatch, comb = slot_tables(where_ref, ids_ref, score_ref)
    comb_ref[...] = comb
    for i, ref in enumerate(tok_refs):
        rows = slice(i * HALF, (i + 1) * HALF)
        picked = dot(dispatch, ref[...]).astype(BF16)
        own_ref[rows] = picked[:HALF]
        far_ref[rows] = picked[HALF:]


def weave_body(own_ref, got_ref, *block_refs):
    own = own_ref[...].astype(F32)
    got = got_ref[...].astype(F32)
    for q, ref in enumerate(block_refs):
        parts = []
        for base in range(0, own.shape[0], HALF):
            rows = slice(base + q * CAP, base + (q + 1) * CAP)
            parts += [own[rows], got[rows]]
        ref[...] = jnp.concatenate(parts, axis=0).astype(BF16)


def part_body(b0, b1, b2, b3, own_ref, far_ref):
    blocks = [b[...].astype(F32) for b in (b0, b1, b2, b3)]
    own_ref[...] = jnp.concatenate([b[:CAP] for b in blocks], axis=0).astype(BF16)
    far_ref[...] = jnp.concatenate([b[CAP:] for b in blocks], axis=0).astype(BF16)


def join_body(*refs):
    refs[-1][...] = jnp.concatenate([r[...] for r in refs[:-1]], axis=0)


def hidden_body(rows_ref, wg_ref, wu_ref, out_ref):
    rows = rows_ref[...]
    gate = dot(rows, wg_ref[...])
    up = dot(rows, wu_ref[...])
    out_ref[...] = (gate * jax.nn.sigmoid(gate) * up).astype(BF16)


def down_body(mine_ref, theirs_ref, wd_ref, wdp_ref, keep_ref, send_ref):
    total = dot(mine_ref[...], wd_ref[...]) + dot(theirs_ref[...], wdp_ref[...])
    keep_ref[...] = total[:HOME]
    send_ref[...] = total[HOME:].astype(BF16)


def finish_body(*refs):
    blocks, pairs = refs[-PAIRS:], refs[:-PAIRS]
    col = 0
    for i in range(0, len(pairs), 2):
        total = pairs[i][...] + pairs[i + 1][...].astype(F32)
        cols = slice(col, col + total.shape[1])
        for q, ref in enumerate(blocks):
            ref[:, cols] = total[q * BLOCK : (q + 1) * BLOCK].astype(BF16)
        col += total.shape[1]


def slopes(rows, wg_ref, wu_ref):
    gate = dot(rows, wg_ref[...])
    up = dot(rows, wu_ref[...])
    sigma = jax.nn.sigmoid(gate)
    return up * sigma * (1.0 + gate * (1.0 - sigma)), gate * sigma


def slope_body(rows_ref, wg_ref, wu_ref, sg_ref, su_ref):
    sg_ref[...], su_ref[...] = slopes(rows_ref[...], wg_ref, wu_ref)


def grad_hidden_body(rows_ref, wd_ref, wdp_ref, mine_ref, send_ref):
    rows = rows_ref[...]
    mine_ref[...] = dot_t(rows, wd_ref[...])
    send_ref[...] = dot_t(rows, wdp_ref[...])


def grads_body(
    sg_ref, su_ref, sgx_ref, sux_ref, mine_ref, got_ref, gg_ref, gu_ref
):
    mine = mine_ref[...]
    got = got_ref[...]
    count = mine.shape[0]
    gg_ref[:count] = (mine * sg_ref[...]).astype(BF16)
    gg_ref[count:] = (got * sgx_ref[...]).astype(BF16)
    gu_ref[:count] = (mine * su_ref[...]).astype(BF16)
    gu_ref[count:] = (got * sux_ref[...]).astype(BF16)


def back_x_body(gg_ref, gu_ref, wg_ref, wu_ref, keep_ref, send_ref):
    total = dot_t(gg_ref[...], wg_ref[...]) + dot_t(gu_ref[...], wu_ref[...])
    count = keep_ref.shape[0]
    keep_ref[...] = total[:count]
    send_ref[...] = total[count:].astype(BF16)


def back_z_body(gg_ref, gu_ref, wg_ref, wu_ref, keep_ref, send_ref):
    total = dot_t(gg_ref[...], wg_ref[...]) + dot_t(gu_ref[...], wu_ref[...])
    keep_ref[:HOME] = total[:HOME]
    keep_ref[HOME:] = total[2 * HOME : 3 * HOME]
    send_ref[:HOME] = total[HOME : 2 * HOME].astype(BF16)
    send_ref[HOME:] = total[3 * HOME :].astype(BF16)


def fold_body(keep_ref, got_ref, own_ref, send_ref):
    total = keep_ref[...] + got_ref[...].astype(F32)
    own_ref[...] = total[:HOME]
    send_ref[...] = total[HOME:].astype(BF16)


def combine_body(base_ref, comb_ref, own_ref, far_ref, out_ref):
    rows = jnp.concatenate([own_ref[...], far_ref[...]], axis=0)
    total = dot(comb_ref[...], jnp.concatenate([rows, rows], axis=0))
    out_ref[...] = (base_ref[...].astype(F32) + total).astype(BF16)


def marked_body(base_ref, comb_ref, own_ref, far_ref, out_ref, mark_ref):
    combine_body(base_ref, comb_ref, own_ref, far_ref, out_ref)
    mark_ref[...] = jnp.zeros_like(mark_ref)


def back_call(body, gg, gu, wg, wu, index, chunks):
    width = wg.shape[0] // chunks
    rows = gg.shape[0]
    whole = pl.BlockSpec((rows, gg.shape[1]), lambda i: (0, 0))
    part = pl.BlockSpec((width, wg.shape[1]), lambda i: (index, 0))
    half = rows // 2
    return pl.pallas_call(
        body,
        grid=(1,),
        out_shape=(shape(half, width, F32), shape(half, width)),
        in_specs=[whole, whole, part, part],
        out_specs=(
            pl.BlockSpec((half, width), lambda i: (0, 0)),
            pl.BlockSpec((half, width), lambda i: (0, 0)),
        ),
        compiler_params=pltpu.CompilerParams(vmem_limit_bytes=48 * 1024 * 1024),
        cost_estimate=pl.CostEstimate(
            flops=4 * rows * width * gg.shape[1],
            bytes_accessed=4 * width * wg.shape[1] + 6 * half * width,
            transcendentals=0,
        ),
    )(gg, gu, wg, wu)


def join(parts, after=()):
    rows = sum(p.shape[0] for p in parts)
    return call(join_body, [shape(rows, parts[0].shape[1])], parts, after=after)[0]


def shifts(blocks, back):
    a, b, c = SHIFT_A, SHIFT_B, SHIFT_C
    if back:
        a, b, c = inverse(a), inverse(b), inverse(c)
    return [blocks[0], move(blocks[1], a), move(blocks[2], b), move(blocks[3], c)]


def per_device(
    fwd_in, fwd_ids, fwd_score, bwd_in, bwd_ids, bwd_score, bwd_cot, w_gate, w_up, w_down
):
    tokens, width = fwd_in.shape[1:]
    wg, wu, wd = w_gate[0], w_up[0], w_down[0]
    hid = wg.shape[1]
    rows = 2 * HOME
    proj = 4 * rows * width * hid
    wdp = move(wd, DP_PAIR)
    where = lax.axis_index("expert").astype(jnp.int32).reshape(1)
    table = shape(tokens, 2 * HOME)

    own, far, fcomb = call(
        pack_body,
        [shape(HALF, width)] * 2 + [table],
        [where, fwd_ids[0].T, fwd_score[0].T, fwd_in[0]],
        smem=(0,),
        limit=60,
    )
    got = move(far, ACROSS_XHI)
    bown, bfar, bcomb = call(
        pack_body,
        [shape(2 * HALF, width)] * 2 + [table],
        [where, bwd_ids[0].T, bwd_score[0].T, bwd_in[0], bwd_cot[0]],
        smem=(0,),
        limit=60,
        after=(got,),
    )
    blocks = call(weave_body, [shape(BLOCK, width)] * PAIRS, [own, got])
    fy = jnp.concatenate(shifts(blocks, False), axis=0)
    bblocks = call(
        weave_body,
        [shape(2 * BLOCK, width)] * PAIRS,
        [bown, move(bfar, ACROSS_XHI)],
        after=(fy,),
    )
    fy = jnp.concatenate([fy, move(fy, Z_PAIR)], axis=0)
    fyx = move(fy, DP_PAIR)
    (mine,) = call(hidden_body, [shape(rows, hid)], [fy, wg, wu], proj)

    bbase = relay(join([bwd_cot[0]], after=(mine,)), STAY, -1)
    bcomb = relay(join([bcomb], after=(mine,)), STAY, -1)
    parts = shifts(bblocks, False)
    by = jnp.concatenate([p[:BLOCK] for p in parts], axis=0)
    cy = jnp.concatenate([p[BLOCK:] for p in parts], axis=0)
    byz = move(by, Z_PAIR)
    cy = jnp.concatenate([cy, move(cy, Z_PAIR)], axis=0)

    (theirs,) = call(hidden_body, [shape(rows, hid)], [fyx, wg, wu], proj, after=(mine,))
    theirs = move(theirs, DP_PAIR)
    by = join([by, byz], after=(theirs,))
    byx = move(by, DP_PAIR)
    keep, send = call(
        down_body, [shape(HOME, width, F32), shape(HOME, width)], [mine, theirs, wd, wdp], proj
    )
    fgot = move(send, Z_PAIR)
    blocks = call(finish_body, [shape(BLOCK, width)] * PAIRS, [keep, fgot])
    fin = blocks[0]
    blocks = shifts(blocks, True)
    sg, su = call(
        slope_body, [shape(rows, hid, F32)] * 2, [by, wg, wu], proj, after=(bcomb,)
    )
    gh, gh_send = call(grad_hidden_body, [shape(rows, hid, F32)] * 2, [cy, wd, wdp], proj)
    gh_got = move(gh_send, DP_PAIR)
    fbase = relay(join([fwd_in[0]], after=(gh_send,)), STAY, 1)
    fcomb = relay(join([fcomb], after=(gh_send,)), STAY, 1)
    sgx, sux = call(
        slope_body,
        [shape(rows, hid, F32)] * 2,
        [byx, wg, wu],
        proj,
        after=(fin, bbase, fcomb),
    )
    gg, gu = call(
        grads_body, [shape(2 * rows, hid)] * 2, [sg, su, sgx, sux, gh, gh_got]
    )
    half = width // 2
    fold = [shape(HOME, half, F32), shape(HOME, half)]
    xkeep, xsend = back_call(back_x_body, gg, gu, wg, wu, 0, 2)
    zkeep, zsend = back_call(back_z_body, gg, gu, wg, wu, 1, 2)
    xgot, zgot = move(xsend, DP_PAIR), move(zsend, Z_PAIR)
    xkeep, xsend = call(fold_body, fold, [xkeep, xgot])
    zkeep, zsend = call(fold_body, fold, [zkeep, zgot])
    own, far = call(
        part_body, [shape(HALF, width)] * 2, blocks, after=(xsend, zsend)
    )
    own, far = relay(own, STAY, 1), relay(far, ACROSS_XHI, 1)
    fwd_out, mark = call(
        marked_body,
        [shape(tokens, width), shape(8, 128, F32)],
        [fbase, fcomb, own, far],
    )
    bbase = join([bbase], after=(xkeep, zkeep))
    xgot, zgot = move(xsend, Z_PAIR), move(zsend, DP_PAIR)
    blocks = call(
        finish_body, [shape(BLOCK, width)] * PAIRS, [xkeep, xgot, zkeep, zgot]
    )
    own, far = call(part_body, [shape(HALF, width)] * 2, shifts(blocks, True))
    own, far = relay(own, STAY, -1), relay(far, ACROSS_XHI, -1)
    (bwd_out,) = call(
        combine_body,
        [shape(tokens, width)],
        [bbase, bcomb, own, far],
        after=(mark,),
    )
    return fwd_out[None], bwd_out[None]


def solution(mesh):
    rows = P("pipe", ("expert", "dp"), None)
    cols = P("pipe", None, ("expert", "dp"))
    return jax.shard_map(
        per_device,
        mesh=mesh,
        in_specs=(rows,) * 7 + (cols, cols, rows),
        out_specs=(rows, rows),
        check_vma=False,
    )
```

```python
import functools

import jax
import jax.numpy as jnp
from jax import lax
from jax.experimental import pallas as pl
from jax.experimental.pallas import tpu as pltpu
from jax.sharding import PartitionSpec as P

CAP = 8
PAIRS = 4
BLOCK = 2 * CAP
HALF = PAIRS * CAP
HOME = PAIRS * BLOCK
BF16 = jnp.bfloat16
F32 = jnp.float32


def call(body, outs, args, flops=0, smem=(), after=(), limit=48):
    total = sum(a.size * a.dtype.itemsize for a in args)
    total += sum(o.size * o.dtype.itemsize for o in outs)
    specs = [
        pl.BlockSpec(memory_space=pltpu.SMEM if i in smem else pltpu.VMEM)
        for i in range(len(args))
    ]
    specs += [pl.BlockSpec(memory_space=pl.ANY)] * len(after)
    used, extra = len(args), len(after)

    def run(*refs):
        body(*refs[:used], *refs[used + extra :])

    return pl.pallas_call(
        run,
        out_shape=tuple(outs),
        in_specs=specs,
        out_specs=tuple(pl.BlockSpec(memory_space=pltpu.VMEM) for _ in outs),
        compiler_params=pltpu.CompilerParams(vmem_limit_bytes=limit * 1024 * 1024),
        cost_estimate=pl.CostEstimate(flops=flops, bytes_accessed=total, transcendentals=0),
    )(*args, *after)


def shape(rows, cols, dtype=BF16):
    return jax.ShapeDtypeStruct((rows, cols), dtype)


def dot(a, b):
    return lax.dot_general(a, b, (((1,), (0,)), ((), ())), preferred_element_type=F32)


def dot_t(a, b):
    return lax.dot_general(a, b, (((1,), (1,)), ((), ())), preferred_element_type=F32)


def section_perm(move):
    pairs = []
    for xh in range(2):
        for z in range(8):
            for d in range(2):
                nxh, nz, nd = move(xh, z, d)
                pairs.append(((xh * 8 + z) * 2 + d, (nxh * 8 + nz % 8) * 2 + nd))
    return pairs


def inverse(pairs):
    return [(b, a) for a, b in pairs]


ACROSS_XHI = section_perm(lambda xh, z, d: (1 - xh, z, 1 - d))
SHIFT_A = section_perm(lambda xh, z, d: (xh, z + (2 if z % 2 == 0 else -2), d))
SHIFT_B = section_perm(lambda xh, z, d: (xh, z + (-1 if z % 2 == 0 else 1), d))
SHIFT_C = section_perm(lambda xh, z, d: (xh, z + (-3 if z % 2 == 0 else 3), d))
Z_PAIR = section_perm(lambda xh, z, d: (xh, z ^ 1, d))
DP_PAIR = section_perm(lambda xh, z, d: (xh, z, 1 - d))
STAY = section_perm(lambda xh, z, d: (xh, z, d))


def move(value, pairs):
    return lax.ppermute(value, ("expert", "dp"), pairs)


def relay(value, pairs, step):
    sections = lax.axis_size("pipe")
    size = len(pairs)
    full = []
    for s in range(sections):
        t = s + step
        if 0 <= t < sections:
            full += [(s * size + a, t * size + b) for a, b in pairs]
    return lax.ppermute(value, ("pipe", "expert", "dp"), full)


def slot_tables(where_ref, ids_ref, score_ref):
    choices, tokens = ids_ref.shape
    where = where_ref[0]
    xh = where // 8
    z = where % 8
    pair = z // 2
    sign = 1 - 2 * (z % 2)
    shape2 = (2 * HOME, tokens)
    index = lax.broadcasted_iota(jnp.int32, shape2, 0)
    slot = index & (HOME - 1)
    half = slot >> 5
    q = (slot >> 3) & 3
    rank_of = slot & 7
    gray = q ^ (q >> 1)
    expert = (xh ^ half) * PAIRS + ((pair + sign * gray) & 3)
    ids = ids_ref[...]
    score = score_ref[...]
    mix = 2.5 * score / jnp.sum(score, axis=0, keepdims=True)
    hit = jnp.zeros(shape2, F32)
    weight = jnp.zeros(shape2, F32)
    for k in range(choices):
        same = ids[k : k + 1] == expert
        hit = jnp.where(same, 1.0, hit)
        weight = jnp.where(same, mix[k : k + 1], weight)
    row = lax.broadcasted_iota(jnp.int32, (tokens, tokens), 0)
    col = lax.broadcasted_iota(jnp.int32, (tokens, tokens), 1)
    before = jnp.where(row < col, 1.0, 0.0).astype(BF16)
    rank = dot(hit.astype(BF16), before)
    taken = jnp.where((hit > 0.0) & (rank == rank_of.astype(F32)), 1.0, 0.0)
    weight = weight * taken
    high = weight.astype(BF16).astype(F32)
    comb = jnp.where(index < HOME, high, weight - high)
    return taken[:HOME].astype(BF16), jnp.transpose(comb).astype(BF16)


def pack_body(where_ref, ids_ref, score_ref, *refs):
    tok_refs, (own_ref, far_ref, comb_ref) = refs[:-3], refs[-3:]
    dispatch, comb = slot_tables(where_ref, ids_ref, score_ref)
    comb_ref[...] = comb
    for i, ref in enumerate(tok_refs):
        rows = slice(i * HALF, (i + 1) * HALF)
        picked = dot(dispatch, ref[...]).astype(BF16)
        own_ref[rows] = picked[:HALF]
        far_ref[rows] = picked[HALF:]


def weave_body(own_ref, got_ref, *block_refs):
    own = own_ref[...].astype(F32)
    got = got_ref[...].astype(F32)
    for q, ref in enumerate(block_refs):
        parts = []
        for base in range(0, own.shape[0], HALF):
            rows = slice(base + q * CAP, base + (q + 1) * CAP)
            parts += [own[rows], got[rows]]
        ref[...] = jnp.concatenate(parts, axis=0).astype(BF16)


def part_body(b0, b1, b2, b3, own_ref, far_ref):
    blocks = [b[...].astype(F32) for b in (b0, b1, b2, b3)]
    own_ref[...] = jnp.concatenate([b[:CAP] for b in blocks], axis=0).astype(BF16)
    far_ref[...] = jnp.concatenate([b[CAP:] for b in blocks], axis=0).astype(BF16)


def side_body(side, b0, b1, b2, b3, out_ref):
    rows = slice(side * CAP, (side + 1) * CAP)
    blocks = [b[...].astype(F32)[rows] for b in (b0, b1, b2, b3)]
    out_ref[...] = jnp.concatenate(blocks, axis=0).astype(BF16)


def join_body(*refs):
    refs[-1][...] = jnp.concatenate([r[...] for r in refs[:-1]], axis=0)


def hidden_body(rows_ref, wg_ref, wu_ref, out_ref):
    rows = rows_ref[...]
    gate = dot(rows, wg_ref[...])
    up = dot(rows, wu_ref[...])
    out_ref[...] = (gate * jax.nn.sigmoid(gate) * up).astype(BF16)


def down_body(mine_ref, theirs_ref, wd_ref, wdp_ref, keep_ref, send_ref):
    total = dot(mine_ref[...], wd_ref[...]) + dot(theirs_ref[...], wdp_ref[...])
    keep_ref[...] = total[:HOME]
    send_ref[...] = total[HOME:].astype(BF16)


def finish_body(*refs):
    blocks, pairs = refs[-PAIRS:], refs[:-PAIRS]
    col = 0
    for i in range(0, len(pairs), 2):
        total = pairs[i][...] + pairs[i + 1][...].astype(F32)
        cols = slice(col, col + total.shape[1])
        for q, ref in enumerate(blocks):
            ref[:, cols] = total[q * BLOCK : (q + 1) * BLOCK].astype(BF16)
        col += total.shape[1]


def slopes(rows, wg_ref, wu_ref):
    gate = dot(rows, wg_ref[...])
    up = dot(rows, wu_ref[...])
    sigma = jax.nn.sigmoid(gate)
    return up * sigma * (1.0 + gate * (1.0 - sigma)), gate * sigma


def slope_body(rows_ref, wg_ref, wu_ref, sg_ref, su_ref):
    sg_ref[...], su_ref[...] = slopes(rows_ref[...], wg_ref, wu_ref)


def grad_hidden_body(rows_ref, wd_ref, wdp_ref, mine_ref, send_ref):
    rows = rows_ref[...]
    mine_ref[...] = dot_t(rows, wd_ref[...])
    send_ref[...] = dot_t(rows, wdp_ref[...]).astype(BF16)


def grads_body(
    sg_ref, su_ref, sgx_ref, sux_ref, mine_ref, got_ref, gg_ref, gu_ref
):
    mine = mine_ref[...]
    got = got_ref[...].astype(F32)
    count = mine.shape[0]
    gg_ref[:count] = (mine * sg_ref[...]).astype(BF16)
    gg_ref[count:] = (got * sgx_ref[...]).astype(BF16)
    gu_ref[:count] = (mine * su_ref[...]).astype(BF16)
    gu_ref[count:] = (got * sux_ref[...]).astype(BF16)


def back_x_body(gg_ref, gu_ref, wg_ref, wu_ref, keep_ref, send_ref):
    total = dot_t(gg_ref[...], wg_ref[...]) + dot_t(gu_ref[...], wu_ref[...])
    count = keep_ref.shape[0]
    keep_ref[...] = total[:count]
    send_ref[...] = total[count:].astype(BF16)


def back_z_body(gg_ref, gu_ref, wg_ref, wu_ref, keep_ref, send_ref):
    total = dot_t(gg_ref[...], wg_ref[...]) + dot_t(gu_ref[...], wu_ref[...])
    keep_ref[:HOME] = total[:HOME]
    keep_ref[HOME:] = total[2 * HOME : 3 * HOME]
    send_ref[:HOME] = total[HOME : 2 * HOME].astype(BF16)
    send_ref[HOME:] = total[3 * HOME :].astype(BF16)


def fold_body(keep_ref, got_ref, own_ref, send_ref):
    total = keep_ref[...] + got_ref[...].astype(F32)
    own_ref[...] = total[:HOME]
    send_ref[...] = total[HOME:].astype(BF16)


def combine_body(base_ref, comb_ref, own_ref, far_ref, out_ref):
    rows = jnp.concatenate([own_ref[...], far_ref[...]], axis=0)
    total = dot(comb_ref[...], jnp.concatenate([rows, rows], axis=0))
    out_ref[...] = (base_ref[...].astype(F32) + total).astype(BF16)


def marked_body(base_ref, comb_ref, own_ref, far_ref, out_ref, mark_ref):
    combine_body(base_ref, comb_ref, own_ref, far_ref, out_ref)
    mark_ref[...] = jnp.zeros_like(mark_ref)


def back_call(body, gg, gu, wg, wu, index, chunks):
    width = wg.shape[0] // chunks
    rows = gg.shape[0]
    whole = pl.BlockSpec((rows, gg.shape[1]), lambda i: (0, 0))
    part = pl.BlockSpec((width, wg.shape[1]), lambda i: (index, 0))
    half = rows // 2
    return pl.pallas_call(
        body,
        grid=(1,),
        out_shape=(shape(half, width, F32), shape(half, width)),
        in_specs=[whole, whole, part, part],
        out_specs=(
            pl.BlockSpec((half, width), lambda i: (0, 0)),
            pl.BlockSpec((half, width), lambda i: (0, 0)),
        ),
        compiler_params=pltpu.CompilerParams(vmem_limit_bytes=48 * 1024 * 1024),
        cost_estimate=pl.CostEstimate(
            flops=4 * rows * width * gg.shape[1],
            bytes_accessed=4 * width * wg.shape[1] + 6 * half * width,
            transcendentals=0,
        ),
    )(gg, gu, wg, wu)


def join(parts, after=()):
    rows = sum(p.shape[0] for p in parts)
    return call(join_body, [shape(rows, parts[0].shape[1])], parts, after=after)[0]


def shifts(blocks, back):
    a, b, c = SHIFT_A, SHIFT_B, SHIFT_C
    if back:
        a, b, c = inverse(a), inverse(b), inverse(c)
    return [blocks[0], move(blocks[1], a), move(blocks[2], b), move(blocks[3], c)]


def per_device(
    fwd_in, fwd_ids, fwd_score, bwd_in, bwd_ids, bwd_score, bwd_cot, w_gate, w_up, w_down
):
    tokens, width = fwd_in.shape[1:]
    wg, wu, wd = w_gate[0], w_up[0], w_down[0]
    hid = wg.shape[1]
    rows = 2 * HOME
    proj = 4 * rows * width * hid
    wdp = move(wd, DP_PAIR)
    where = lax.axis_index("expert").astype(jnp.int32).reshape(1)
    table = shape(tokens, 2 * HOME)

    own, far, fcomb = call(
        pack_body,
        [shape(HALF, width)] * 2 + [table],
        [where, fwd_ids[0].T, fwd_score[0].T, fwd_in[0]],
        smem=(0,),
        limit=60,
    )
    got = move(far, ACROSS_XHI)
    bown, bfar, bcomb = call(
        pack_body,
        [shape(2 * HALF, width)] * 2 + [table],
        [where, bwd_ids[0].T, bwd_score[0].T, bwd_in[0], bwd_cot[0]],
        smem=(0,),
        limit=60,
        after=(got,),
    )
    blocks = call(weave_body, [shape(BLOCK, width)] * PAIRS, [own, got])
    fy = jnp.concatenate(shifts(blocks, False), axis=0)
    bblocks = call(
        weave_body,
        [shape(2 * BLOCK, width)] * PAIRS,
        [bown, move(bfar, ACROSS_XHI)],
        after=(fy,),
    )
    fy = jnp.concatenate([fy, move(fy, Z_PAIR)], axis=0)
    fyx = move(fy, DP_PAIR)
    (mine,) = call(hidden_body, [shape(rows, hid)], [fy, wg, wu], proj)

    bbase = relay(join([bwd_cot[0]], after=(mine,)), STAY, -1)
    bcomb = relay(join([bcomb], after=(mine,)), STAY, -1)
    parts = shifts(bblocks, False)
    by = jnp.concatenate([p[:BLOCK] for p in parts], axis=0)
    cy = jnp.concatenate([p[BLOCK:] for p in parts], axis=0)
    byz = move(by, Z_PAIR)
    cy = jnp.concatenate([cy, move(cy, Z_PAIR)], axis=0)

    (theirs,) = call(hidden_body, [shape(rows, hid)], [fyx, wg, wu], proj, after=(mine,))
    theirs = move(theirs, DP_PAIR)
    by = join([by, byz], after=(theirs,))
    byx = move(by, DP_PAIR)
    keep, send = call(
        down_body, [shape(HOME, width, F32), shape(HOME, width)], [mine, theirs, wd, wdp], proj
    )
    fgot = move(send, Z_PAIR)
    blocks = call(finish_body, [shape(BLOCK, width)] * PAIRS, [keep, fgot])
    fin = blocks[0]
    blocks = shifts(blocks, True)
    sg, su = call(
        slope_body, [shape(rows, hid, F32)] * 2, [by, wg, wu], proj, after=(bcomb,)
    )
    gh, gh_send = call(
        grad_hidden_body,
        [shape(rows, hid, F32), shape(rows, hid)],
        [cy, wd, wdp],
        proj,
    )
    gh_got = move(gh_send, DP_PAIR)
    fbase = relay(join([fwd_in[0]], after=(gh_send,)), STAY, 1)
    fcomb = relay(join([fcomb], after=(gh_send,)), STAY, 1)
    sgx, sux = call(
        slope_body,
        [shape(rows, hid, F32)] * 2,
        [byx, wg, wu],
        proj,
        after=(fin, bbase, fcomb),
    )
    gg, gu = call(
        grads_body, [shape(2 * rows, hid)] * 2, [sg, su, sgx, sux, gh, gh_got]
    )
    half = width // 2
    fold = [shape(HOME, half, F32), shape(HOME, half)]
    xkeep, xsend = back_call(back_x_body, gg, gu, wg, wu, 0, 2)
    zkeep, zsend = back_call(back_z_body, gg, gu, wg, wu, 1, 2)
    xgot, zgot = move(xsend, DP_PAIR), move(zsend, Z_PAIR)
    xkeep, xsend = call(fold_body, fold, [xkeep, xgot])
    zkeep, zsend = call(fold_body, fold, [zkeep, zgot])
    own, far = call(
        part_body, [shape(HALF, width)] * 2, blocks, after=(xsend, zsend)
    )
    own, far = relay(own, STAY, 1), relay(far, ACROSS_XHI, 1)
    fwd_out, mark = call(
        marked_body,
        [shape(tokens, width), shape(8, 128, F32)],
        [fbase, fcomb, own, far],
    )
    bbase = join([bbase], after=(xkeep, zkeep))
    xgot, zgot = move(xsend, Z_PAIR), move(zsend, DP_PAIR)
    blocks = call(
        finish_body, [shape(BLOCK, width)] * PAIRS, [xkeep, xgot, zkeep, zgot]
    )
    blocks = shifts(blocks, True)
    (far,) = call(functools.partial(side_body, 1), [shape(HALF, width)], blocks)
    (own,) = call(
        functools.partial(side_body, 0), [shape(HALF, width)], blocks, after=(far,)
    )
    far, own = relay(far, ACROSS_XHI, -1), relay(own, STAY, -1)
    (bwd_out,) = call(
        combine_body,
        [shape(tokens, width)],
        [bbase, bcomb, own, far],
        after=(mark,),
    )
    return fwd_out[None], bwd_out[None]


def solution(mesh):
    rows = P("pipe", ("expert", "dp"), None)
    cols = P("pipe", None, ("expert", "dp"))
    return jax.shard_map(
        per_device,
        mesh=mesh,
        in_specs=(rows,) * 7 + (cols, cols, rows),
        out_specs=(rows, rows),
        check_vma=False,
    )
```

```python
import functools

import jax
import jax.numpy as jnp
from jax import lax
from jax.experimental import pallas as pl
from jax.experimental.pallas import tpu as pltpu
from jax.sharding import PartitionSpec as P

CAP = 8
PAIRS = 4
BLOCK = 2 * CAP
HALF = PAIRS * CAP
HOME = PAIRS * BLOCK
BF16 = jnp.bfloat16
F32 = jnp.float32


def call(body, outs, args, flops=0, smem=(), after=(), limit=48):
    total = sum(a.size * a.dtype.itemsize for a in args)
    total += sum(o.size * o.dtype.itemsize for o in outs)
    specs = [
        pl.BlockSpec(memory_space=pltpu.SMEM if i in smem else pltpu.VMEM)
        for i in range(len(args))
    ]
    specs += [pl.BlockSpec(memory_space=pl.ANY)] * len(after)
    used, extra = len(args), len(after)

    def run(*refs):
        body(*refs[:used], *refs[used + extra :])

    return pl.pallas_call(
        run,
        out_shape=tuple(outs),
        in_specs=specs,
        out_specs=tuple(pl.BlockSpec(memory_space=pltpu.VMEM) for _ in outs),
        compiler_params=pltpu.CompilerParams(vmem_limit_bytes=limit * 1024 * 1024),
        cost_estimate=pl.CostEstimate(flops=flops, bytes_accessed=total, transcendentals=0),
    )(*args, *after)


def shape(rows, cols, dtype=BF16):
    return jax.ShapeDtypeStruct((rows, cols), dtype)


def dot(a, b):
    return lax.dot_general(a, b, (((1,), (0,)), ((), ())), preferred_element_type=F32)


def dot_t(a, b):
    return lax.dot_general(a, b, (((1,), (1,)), ((), ())), preferred_element_type=F32)


def section_perm(move):
    pairs = []
    for xh in range(2):
        for z in range(8):
            for d in range(2):
                nxh, nz, nd = move(xh, z, d)
                pairs.append(((xh * 8 + z) * 2 + d, (nxh * 8 + nz % 8) * 2 + nd))
    return pairs


def inverse(pairs):
    return [(b, a) for a, b in pairs]


ACROSS_XHI = section_perm(lambda xh, z, d: (1 - xh, z, 1 - d))
SHIFT_A = section_perm(lambda xh, z, d: (xh, z + (2 if z % 2 == 0 else -2), d))
SHIFT_B = section_perm(lambda xh, z, d: (xh, z + (-1 if z % 2 == 0 else 1), d))
SHIFT_C = section_perm(lambda xh, z, d: (xh, z + (-3 if z % 2 == 0 else 3), d))
Z_PAIR = section_perm(lambda xh, z, d: (xh, z ^ 1, d))
DP_PAIR = section_perm(lambda xh, z, d: (xh, z, 1 - d))
STAY = section_perm(lambda xh, z, d: (xh, z, d))


def move(value, pairs):
    return lax.ppermute(value, ("expert", "dp"), pairs)


def relay(value, pairs, step):
    sections = lax.axis_size("pipe")
    size = len(pairs)
    full = []
    for s in range(sections):
        t = s + step
        if 0 <= t < sections:
            full += [(s * size + a, t * size + b) for a, b in pairs]
    return lax.ppermute(value, ("pipe", "expert", "dp"), full)


def slot_tables(where_ref, ids_ref, score_ref):
    choices, tokens = ids_ref.shape
    where = where_ref[0]
    xh = where // 8
    z = where % 8
    pair = z // 2
    sign = 1 - 2 * (z % 2)
    shape2 = (2 * HOME, tokens)
    index = lax.broadcasted_iota(jnp.int32, shape2, 0)
    slot = index & (HOME - 1)
    half = slot >> 5
    q = (slot >> 3) & 3
    rank_of = slot & 7
    gray = q ^ (q >> 1)
    expert = (xh ^ half) * PAIRS + ((pair + sign * gray) & 3)
    ids = ids_ref[...]
    score = score_ref[...]
    mix = 2.5 * score / jnp.sum(score, axis=0, keepdims=True)
    hit = jnp.zeros(shape2, F32)
    weight = jnp.zeros(shape2, F32)
    for k in range(choices):
        same = ids[k : k + 1] == expert
        hit = jnp.where(same, 1.0, hit)
        weight = jnp.where(same, mix[k : k + 1], weight)
    row = lax.broadcasted_iota(jnp.int32, (tokens, tokens), 0)
    col = lax.broadcasted_iota(jnp.int32, (tokens, tokens), 1)
    before = jnp.where(row < col, 1.0, 0.0).astype(BF16)
    rank = dot(hit.astype(BF16), before)
    taken = jnp.where((hit > 0.0) & (rank == rank_of.astype(F32)), 1.0, 0.0)
    weight = weight * taken
    high = weight.astype(BF16).astype(F32)
    comb = jnp.where(index < HOME, high, weight - high)
    return taken[:HOME].astype(BF16), jnp.transpose(comb).astype(BF16)


def pack_body(where_ref, ids_ref, score_ref, *refs):
    tok_refs, (own_ref, far_ref, comb_ref) = refs[:-3], refs[-3:]
    dispatch, comb = slot_tables(where_ref, ids_ref, score_ref)
    comb_ref[...] = comb
    for i, ref in enumerate(tok_refs):
        rows = slice(i * HALF, (i + 1) * HALF)
        picked = dot(dispatch, ref[...]).astype(BF16)
        own_ref[rows] = picked[:HALF]
        far_ref[rows] = picked[HALF:]


def weave_body(own_ref, got_ref, *block_refs):
    own = own_ref[...].astype(F32)
    got = got_ref[...].astype(F32)
    for q, ref in enumerate(block_refs):
        parts = []
        for base in range(0, own.shape[0], HALF):
            rows = slice(base + q * CAP, base + (q + 1) * CAP)
            parts += [own[rows], got[rows]]
        ref[...] = jnp.concatenate(parts, axis=0).astype(BF16)


def part_body(b0, b1, b2, b3, own_ref, far_ref):
    blocks = [b[...].astype(F32) for b in (b0, b1, b2, b3)]
    own_ref[...] = jnp.concatenate([b[:CAP] for b in blocks], axis=0).astype(BF16)
    far_ref[...] = jnp.concatenate([b[CAP:] for b in blocks], axis=0).astype(BF16)


def side_body(side, b0, b1, b2, b3, out_ref):
    rows = slice(side * CAP, (side + 1) * CAP)
    blocks = [b[...].astype(F32)[rows] for b in (b0, b1, b2, b3)]
    out_ref[...] = jnp.concatenate(blocks, axis=0).astype(BF16)


def join_body(*refs):
    refs[-1][...] = jnp.concatenate([r[...] for r in refs[:-1]], axis=0)


def hidden_body(rows_ref, wg_ref, wu_ref, out_ref):
    rows = rows_ref[...]
    gate = dot(rows, wg_ref[...])
    up = dot(rows, wu_ref[...])
    out_ref[...] = (gate * jax.nn.sigmoid(gate) * up).astype(BF16)


def down_body(mine_ref, theirs_ref, wd_ref, wdp_ref, keep_ref, send_ref):
    total = dot(mine_ref[...], wd_ref[...]) + dot(theirs_ref[...], wdp_ref[...])
    keep_ref[...] = total[:HOME]
    send_ref[...] = total[HOME:].astype(BF16)


def finish_body(*refs):
    blocks, pairs = refs[-PAIRS:], refs[:-PAIRS]
    col = 0
    for i in range(0, len(pairs), 2):
        total = pairs[i][...] + pairs[i + 1][...].astype(F32)
        cols = slice(col, col + total.shape[1])
        for q, ref in enumerate(blocks):
            ref[:, cols] = total[q * BLOCK : (q + 1) * BLOCK].astype(BF16)
        col += total.shape[1]


def slopes(rows, wg_ref, wu_ref):
    gate = dot(rows, wg_ref[...])
    up = dot(rows, wu_ref[...])
    sigma = jax.nn.sigmoid(gate)
    return up * sigma * (1.0 + gate * (1.0 - sigma)), gate * sigma


def slope_body(rows_ref, wg_ref, wu_ref, sg_ref, su_ref):
    sg_ref[...], su_ref[...] = slopes(rows_ref[...], wg_ref, wu_ref)


def grad_hidden_body(rows_ref, wd_ref, wdp_ref, mine_ref, send_ref):
    rows = rows_ref[...]
    mine_ref[...] = dot_t(rows, wd_ref[...])
    send_ref[...] = dot_t(rows, wdp_ref[...]).astype(BF16)


def grads_body(
    sg_ref, su_ref, sgx_ref, sux_ref, mine_ref, got_ref, gg_ref, gu_ref
):
    mine = mine_ref[...]
    got = got_ref[...].astype(F32)
    count = mine.shape[0]
    gg_ref[:count] = (mine * sg_ref[...]).astype(BF16)
    gg_ref[count:] = (got * sgx_ref[...]).astype(BF16)
    gu_ref[:count] = (mine * su_ref[...]).astype(BF16)
    gu_ref[count:] = (got * sux_ref[...]).astype(BF16)


def back_x_body(gg_ref, gu_ref, wg_ref, wu_ref, keep_ref, send_ref):
    total = dot_t(gg_ref[...], wg_ref[...]) + dot_t(gu_ref[...], wu_ref[...])
    count = keep_ref.shape[0]
    keep_ref[...] = total[:count]
    send_ref[...] = total[count:].astype(BF16)


def back_z_body(gg_ref, gu_ref, wg_ref, wu_ref, keep_ref, send_ref):
    total = dot_t(gg_ref[...], wg_ref[...]) + dot_t(gu_ref[...], wu_ref[...])
    keep_ref[:HOME] = total[:HOME]
    keep_ref[HOME:] = total[2 * HOME : 3 * HOME]
    send_ref[:HOME] = total[HOME : 2 * HOME].astype(BF16)
    send_ref[HOME:] = total[3 * HOME :].astype(BF16)


def fold_body(keep_ref, got_ref, own_ref, send_ref):
    total = keep_ref[...] + got_ref[...].astype(F32)
    own_ref[...] = total[:HOME]
    send_ref[...] = total[HOME:].astype(BF16)


def combine_body(base_ref, comb_ref, own_ref, far_ref, out_ref):
    rows = jnp.concatenate([own_ref[...], far_ref[...]], axis=0)
    total = dot(comb_ref[...], jnp.concatenate([rows, rows], axis=0))
    out_ref[...] = (base_ref[...].astype(F32) + total).astype(BF16)


def marked_body(base_ref, comb_ref, own_ref, far_ref, out_ref, mark_ref):
    combine_body(base_ref, comb_ref, own_ref, far_ref, out_ref)
    mark_ref[...] = jnp.zeros_like(mark_ref)


def back_call(body, gg, gu, wg, wu, index, chunks):
    width = wg.shape[0] // chunks
    rows = gg.shape[0]
    whole = pl.BlockSpec((rows, gg.shape[1]), lambda i: (0, 0))
    part = pl.BlockSpec((width, wg.shape[1]), lambda i: (index, 0))
    half = rows // 2
    return pl.pallas_call(
        body,
        grid=(1,),
        out_shape=(shape(half, width, F32), shape(half, width)),
        in_specs=[whole, whole, part, part],
        out_specs=(
            pl.BlockSpec((half, width), lambda i: (0, 0)),
            pl.BlockSpec((half, width), lambda i: (0, 0)),
        ),
        compiler_params=pltpu.CompilerParams(vmem_limit_bytes=48 * 1024 * 1024),
        cost_estimate=pl.CostEstimate(
            flops=4 * rows * width * gg.shape[1],
            bytes_accessed=4 * width * wg.shape[1] + 6 * half * width,
            transcendentals=0,
        ),
    )(gg, gu, wg, wu)


def join(parts, after=()):
    rows = sum(p.shape[0] for p in parts)
    return call(join_body, [shape(rows, parts[0].shape[1])], parts, after=after)[0]


def combine_call(base, comb, own, far, mark):
    rows, width = base.shape
    part = width // 2

    def run(base_ref, comb_ref, own_ref, far_ref, mark_ref, out_ref):
        combine_body(base_ref, comb_ref, own_ref, far_ref, out_ref)

    def columns(count):
        return pl.BlockSpec((count, part), lambda i: (0, i))

    return pl.pallas_call(
        run,
        grid=(2,),
        out_shape=shape(rows, width),
        in_specs=[
            columns(rows),
            pl.BlockSpec(comb.shape, lambda i: (0, 0)),
            columns(HALF),
            columns(HALF),
            pl.BlockSpec(memory_space=pl.ANY),
        ],
        out_specs=columns(rows),
        compiler_params=pltpu.CompilerParams(vmem_limit_bytes=48 * 1024 * 1024),
        cost_estimate=pl.CostEstimate(
            flops=0, bytes_accessed=6 * rows * width, transcendentals=0
        ),
    )(base, comb, own, far, mark)


def shifts(blocks, back):
    a, b, c = SHIFT_A, SHIFT_B, SHIFT_C
    if back:
        a, b, c = inverse(a), inverse(b), inverse(c)
    return [blocks[0], move(blocks[1], a), move(blocks[2], b), move(blocks[3], c)]


def per_device(
    fwd_in, fwd_ids, fwd_score, bwd_in, bwd_ids, bwd_score, bwd_cot, w_gate, w_up, w_down
):
    tokens, width = fwd_in.shape[1:]
    wg, wu, wd = w_gate[0], w_up[0], w_down[0]
    hid = wg.shape[1]
    rows = 2 * HOME
    proj = 4 * rows * width * hid
    wdp = move(wd, DP_PAIR)
    where = lax.axis_index("expert").astype(jnp.int32).reshape(1)
    table = shape(tokens, 2 * HOME)

    own, far, fcomb = call(
        pack_body,
        [shape(HALF, width)] * 2 + [table],
        [where, fwd_ids[0].T, fwd_score[0].T, fwd_in[0]],
        smem=(0,),
        limit=60,
    )
    got = move(far, ACROSS_XHI)
    bown, bfar, bcomb = call(
        pack_body,
        [shape(2 * HALF, width)] * 2 + [table],
        [where, bwd_ids[0].T, bwd_score[0].T, bwd_in[0], bwd_cot[0]],
        smem=(0,),
        limit=60,
        after=(got,),
    )
    blocks = call(weave_body, [shape(BLOCK, width)] * PAIRS, [own, got])
    fy = jnp.concatenate(shifts(blocks, False), axis=0)
    bblocks = call(
        weave_body,
        [shape(2 * BLOCK, width)] * PAIRS,
        [bown, move(bfar, ACROSS_XHI)],
        after=(fy,),
    )
    fy = jnp.concatenate([fy, move(fy, Z_PAIR)], axis=0)
    fyx = move(fy, DP_PAIR)
    (mine,) = call(hidden_body, [shape(rows, hid)], [fy, wg, wu], proj)

    bbase = relay(join([bwd_cot[0]], after=(mine,)), STAY, -1)
    bcomb = relay(join([bcomb], after=(mine,)), STAY, -1)
    parts = shifts(bblocks, False)
    by = jnp.concatenate([p[:BLOCK] for p in parts], axis=0)
    cy = jnp.concatenate([p[BLOCK:] for p in parts], axis=0)
    byz = move(by, Z_PAIR)
    cy = jnp.concatenate([cy, move(cy, Z_PAIR)], axis=0)

    (theirs,) = call(hidden_body, [shape(rows, hid)], [fyx, wg, wu], proj, after=(mine,))
    theirs = move(theirs, DP_PAIR)
    by = join([by, byz], after=(theirs,))
    byx = move(by, DP_PAIR)
    keep, send = call(
        down_body, [shape(HOME, width, F32), shape(HOME, width)], [mine, theirs, wd, wdp], proj
    )
    fgot = move(send, Z_PAIR)
    blocks = call(finish_body, [shape(BLOCK, width)] * PAIRS, [keep, fgot])
    fin = blocks[0]
    blocks = shifts(blocks, True)
    sg, su = call(
        slope_body, [shape(rows, hid, F32)] * 2, [by, wg, wu], proj, after=(bcomb,)
    )
    gh, gh_send = call(
        grad_hidden_body,
        [shape(rows, hid, F32), shape(rows, hid)],
        [cy, wd, wdp],
        proj,
    )
    gh_got = move(gh_send, DP_PAIR)
    fbase = relay(join([fwd_in[0]], after=(gh_send,)), STAY, 1)
    fcomb = relay(join([fcomb], after=(gh_send,)), STAY, 1)
    sgx, sux = call(
        slope_body,
        [shape(rows, hid, F32)] * 2,
        [byx, wg, wu],
        proj,
        after=(fin, bbase, fcomb),
    )
    gg, gu = call(
        grads_body, [shape(2 * rows, hid)] * 2, [sg, su, sgx, sux, gh, gh_got]
    )
    half = width // 2
    fold = [shape(HOME, half, F32), shape(HOME, half)]
    xkeep, xsend = back_call(back_x_body, gg, gu, wg, wu, 0, 2)
    zkeep, zsend = back_call(back_z_body, gg, gu, wg, wu, 1, 2)
    xgot, zgot = move(xsend, DP_PAIR), move(zsend, Z_PAIR)
    xkeep, xsend = call(fold_body, fold, [xkeep, xgot])
    zkeep, zsend = call(fold_body, fold, [zkeep, zgot])
    own, far = call(
        part_body, [shape(HALF, width)] * 2, blocks, after=(xsend, zsend)
    )
    own, far = relay(own, STAY, 1), relay(far, ACROSS_XHI, 1)
    fwd_out, mark = call(
        marked_body,
        [shape(tokens, width), shape(8, 128, F32)],
        [fbase, fcomb, own, far],
    )
    bbase = join([bbase], after=(xkeep, zkeep))
    xgot, zgot = move(xsend, Z_PAIR), move(zsend, DP_PAIR)
    blocks = call(
        finish_body, [shape(BLOCK, width)] * PAIRS, [xkeep, xgot, zkeep, zgot]
    )
    blocks = shifts(blocks, True)
    (far,) = call(functools.partial(side_body, 1), [shape(HALF, width)], blocks)
    (own,) = call(
        functools.partial(side_body, 0), [shape(HALF, width)], blocks, after=(far,)
    )
    far, own = relay(far, ACROSS_XHI, -1), relay(own, STAY, -1)
    bwd_out = combine_call(bbase, bcomb, own, far, mark)
    return fwd_out[None], bwd_out[None]


def solution(mesh):
    rows = P("pipe", ("expert", "dp"), None)
    cols = P("pipe", None, ("expert", "dp"))
    return jax.shard_map(
        per_device,
        mesh=mesh,
        in_specs=(rows,) * 7 + (cols, cols, rows),
        out_specs=(rows, rows),
        check_vma=False,
    )
```
